256 devices in a mesh: gx: 16 (over z, core), gy: 16 (over y, x).
Axes of the slice: x: 4, y: 4, z: 8, core: 2. Of those that a mesh axis runs over, the one named last changes fastest.
Arguments:
- embeddings: bfloat16 [262144, 4096], P(('gx', 'gy')), may hold values from -100 to 100
- sketch: bfloat16 [4096, 256], replicated, may hold values from -0.09375 to 0.09375
Outputs:
- basis: bfloat16 [262144, 256], P(('gx', 'gy'))
- factor: float32 [256, 256], replicated
- projection: float32 [256, 4096], P('gx', 'gy')
The draws below stay inside these ranges and needn't reach their ends.
All inputs are finite; a program needn't handle non-finite values.
Results may differ from the reference program's by a relative error of at most 0.0013.
Values sent between devices are 32-bit elements; how exact they have to be, the bound alone decides.
No kernel may reach another device: no remote copies, remote signals or barrier semaphores. Data moves between devices by JAX's collectives and lax.ppermute only.
A program may use at most 128 MiB of HBM per device.

```python
import jax
import jax.numpy as jnp
from jax import lax

D = 4096
K = 256
ROWS_DEV = 1024
ROWS = 262144


def draw_embeddings(key, part):
    key = jax.random.fold_in(key, 11)
    key_base, key_rows, key_cols, key_pick = jax.random.split(key, 4)
    base = jax.random.truncated_normal(key_base, -4.0, 4.0, (ROWS, D), jnp.float32)
    place = jnp.arange(ROWS, dtype=jnp.float32)[:, None] / ROWS
    row_scale = jnp.exp(jax.random.uniform(key_rows, (ROWS, 1), jnp.float32, jnp.log(0.3), jnp.log(3.0))) * (0.5 + place)
    col_scale = jnp.exp(jax.random.uniform(key_cols, (1, D), jnp.float32, jnp.log(0.3), jnp.log(3.0)))
    blocks = ROWS // ROWS_DEV
    picked = jax.random.randint(key_pick, (blocks,), 0, 16)
    row_block = jnp.arange(ROWS) // ROWS_DEV
    col_block = jnp.arange(D) // (D // 16)
    boost = jnp.where(col_block[None, :] == picked[row_block][:, None], 4.0, 1.0)
    values = jnp.clip(base * row_scale * col_scale * boost, -100.0, 100.0)
    return values.astype(jnp.bfloat16)


def scatter_about(key, shape, deviation, bound, kind=jnp.bfloat16):
    result = jax.random.normal(key, shape, jnp.float32) * deviation
    return jnp.minimum(jnp.maximum(result, -bound), bound).astype(kind)


def setup_inputs(seed: int = 0) -> dict:
    keys = jax.random.split(jax.random.key(seed), 3)
    return {
        "embeddings": draw_embeddings(jax.random.fold_in(keys[2], 71), 0),
        "sketch": scatter_about(keys[1], (D, K), D ** -0.5, 0.09375),
    }


def matmul_high(left, right):
    return jnp.dot(left, right, precision=lax.Precision.HIGHEST, preferred_element_type=jnp.float32)

def chol_pair(matrix):
    size = matrix.shape[0]
    if size == 1:
        root = jnp.sqrt(matrix)
        return (root, 1.0 / root)
    half = size // 2
    lower_a, inverse_a = chol_pair(matrix[:half, :half])
    below = matmul_high(matrix[half:, :half], inverse_a.T)
    rest = matrix[half:, half:] - matmul_high(below, below.T)
    lower_b, inverse_b = chol_pair(rest)
    zeros_top = jnp.zeros((half, size - half), jnp.float32)
    lower = jnp.concatenate([jnp.concatenate([lower_a, zeros_top], axis=1), jnp.concatenate([below, lower_b], axis=1)], axis=0)
    cross = -matmul_high(inverse_b, matmul_high(below, inverse_a))
    inverse = jnp.concatenate([jnp.concatenate([inverse_a, zeros_top], axis=1), jnp.concatenate([cross, inverse_b], axis=1)], axis=0)
    return (lower, inverse)

def reference(embeddings, sketch):
    total_rows = embeddings.shape[0]
    sketched = jnp.dot(embeddings, sketch, preferred_element_type=jnp.float32)
    gram = lax.dot_general(sketched, sketched, (((0,), (0,)), ((), ())), precision=lax.Precision.HIGHEST, preferred_element_type=jnp.float32) / total_rows
    lower, inverse = chol_pair(gram)
    factor = lower.T
    basis = matmul_high(sketched, inverse.T).astype(jnp.bfloat16)
    projection = lax.dot_general(basis, embeddings, (((0,), (0,)), ((), ())), preferred_element_type=jnp.float32) / total_rows
    return (basis, factor, projection)
```

```python
import functools

import jax
import jax.numpy as jnp
from jax import lax
from jax.experimental import pallas as pl
from jax.experimental.pallas import tpu as pltpu
from jax.sharding import PartitionSpec as P

HIGH = lax.Precision.HIGHEST
F32 = jnp.float32


def dot(left, right, left_dim=1, right_dim=0):
    return lax.dot_general(
        left, right, (((left_dim,), (right_dim,)), ((), ())), precision=HIGH, preferred_element_type=F32
    )


def eliminate(pair, size):
    rows = lax.broadcasted_iota(jnp.int32, (size, 1), 0)
    for j in range(0, size, 2):
        u, v = pair[j : j + 1, :], pair[j + 1 : j + 2, :]
        col_u, col_v = pair[:, j : j + 1], pair[:, j + 1 : j + 2]
        a, b, c = u[:, j : j + 1], u[:, j + 1 : j + 2], v[:, j + 1 : j + 2]
        ratio = b * (1.0 / a)
        second = v - u * ratio
        scale = 1.0 / (c - b * ratio)
        below = rows > j + 1
        first = u * (1.0 / a)
        step = jnp.where(below, col_u, 0.0) * first
        step += jnp.where(below, col_v - col_u * ratio, 0.0) * (second * scale)
        pair = jnp.where(rows == j + 1, second, pair - step)
    return pair


def factor_kernel(gram_ref, factor_ref, inverse_ref, work, *, size, block):
    work[...] = gram_ref[...]
    row = lax.broadcasted_iota(jnp.int32, (block, block), 0)
    col = lax.broadcasted_iota(jnp.int32, (block, block), 1)
    eye = (row == col).astype(F32)
    for k in range(size // block):
        lo, hi = k * block, (k + 1) * block
        pair = eliminate(jnp.concatenate([work[lo:hi, lo:hi], eye], axis=1), block)
        diagonal = jnp.sum(jnp.where(row == col, pair[:, :block], 0.0), axis=1, keepdims=True)
        pair = pair * (1.0 / jnp.sqrt(diagonal))
        small = pair[:, block:]
        corner = jnp.where(row <= col, pair[:, :block], 0.0)
        wide = dot(small, work[lo:hi, :])
        left = [wide[:, :lo]] if lo else []
        right = [wide[:, hi:]] if hi < size else []
        pad_left = [jnp.zeros((block, lo), F32)] if lo else []
        pad_right = [jnp.zeros((block, size - hi), F32)] if hi < size else []
        factor_ref[lo:hi, :] = jnp.concatenate(pad_left + [corner] + right, axis=1)
        inverse_ref[lo:hi, :] = jnp.concatenate(left + [small] + pad_right, axis=1)
        if hi < size:
            wide = jnp.concatenate(left + [small] + right, axis=1)
            tall = dot(work[hi:, lo:hi], small, 1, 1)
            lane = lax.broadcasted_iota(jnp.int32, (size - hi, size), 1)
            old = jnp.where((lane >= lo) & (lane < hi), 0.0, work[hi:, :])
            work[hi:, :] = old - dot(tall, wide)


def factorize(gram):
    size = gram.shape[0]
    shape = jax.ShapeDtypeStruct((size, size), F32)
    return pl.pallas_call(
        functools.partial(factor_kernel, size=size, block=64),
        out_shape=(shape, shape),
        scratch_shapes=[pltpu.VMEM((size, size), F32)],
        name="factorize",
    )(gram)


def swap(value, axis, mask):
    return lax.ppermute(value, axis, [(s, s ^ mask) for s in range(lax.axis_size(axis))])


def halve(value, axis, mask, dim=0):
    bit = (lax.axis_index(axis) // mask) % 2
    shape = value.shape
    parts = value.reshape(shape[:dim] + (2, shape[dim] // 2) + shape[dim + 1 :])
    keep = lax.dynamic_index_in_dim(parts, bit, dim, keepdims=False)
    send = lax.dynamic_index_in_dim(parts, 1 - bit, dim, keepdims=False)
    return keep + swap(send, axis, mask)


def double(value, axis, mask):
    bit = (lax.axis_index(axis) // mask) % 2
    other = swap(value, axis, mask)
    return jnp.where(bit == 1, jnp.concatenate([other, value]), jnp.concatenate([value, other]))


def sum_gram(gram):
    split = [("gx", 1), ("gy", 1), ("gy", 2), ("gy", 4), ("gy", 8)]
    for axis, mask in split:
        gram = halve(gram, axis, mask)
    for mask in (2, 4, 8):
        gram = gram + swap(gram, "gx", mask)
    for axis, mask in split[::-1]:
        gram = double(gram, axis, mask)
    return gram


def sum_terms(term):
    blocks, rows, width = term.shape
    first = term[:, : rows // 2].reshape(4, 4, rows // 2, width)
    second = term[:, rows // 2 :].reshape(4, 4, rows // 2, width)
    first = halve(first, "gy", 2, 1)
    second = halve(second, "gy", 8, 0)
    first = halve(first, "gy", 1, 1)
    second = halve(second, "gy", 4, 0)
    first = halve(first, "gy", 8, 0)
    second = halve(second, "gy", 2, 1)
    first = halve(first, "gy", 4, 0)
    second = halve(second, "gy", 1, 1)
    both = jnp.concatenate([first[0, 0], second[0, 0]], axis=0)
    for mask in (2, 4, 8):
        both = halve(both, "gx", mask)
    for mask in (8, 4, 2, 1):
        both = double(both, "gx", mask)
    return both


def body(embeddings, sketch):
    total_rows = embeddings.shape[0] * lax.axis_size("gx") * lax.axis_size("gy")
    rank, width = sketch.shape[1], embeddings.shape[1]
    core = lax.axis_index("gx") % 2
    sketched = jnp.dot(embeddings, sketch, preferred_element_type=F32)
    gram = sum_gram(dot(sketched, sketched, 0, 0) / total_rows)

    high = sketched.astype(jnp.bfloat16)
    low = (sketched - high.astype(F32)).astype(jnp.bfloat16)

    def term(which):
        start = which * (rank // 2)
        two = jnp.concatenate(
            [lax.dynamic_slice_in_dim(part, start, rank // 2, 1) for part in (high, low)], axis=1
        )
        out = lax.dot_general(two, embeddings, (((0,), (0,)), ((), ())), preferred_element_type=F32)
        out = out[: rank // 2] + out[rank // 2 :]
        return out.reshape(rank // 2, 16, width // 16).transpose(1, 0, 2)

    away = swap(term(1 - core), "gx", 1)
    summed = sum_terms(term(core) + away)

    factor, inverse = factorize(gram)
    basis = dot(sketched, inverse, 1, 1).astype(jnp.bfloat16)
    row_count = rank // lax.axis_size("gx")
    mine = lax.dynamic_slice_in_dim(inverse, lax.axis_index("gx") * row_count, row_count, 0)
    projection = dot(mine, summed) / total_rows
    return (basis, factor, projection)


def solution(mesh):
    placed = (P(("gx", "gy"), None), P())
    return jax.shard_map(
        body,
        mesh=mesh,
        in_specs=placed,
        out_specs=(P(("gx", "gy"), None), P(), P("gx", "gy")),
        check_vma=False,
    )
```

```python
import functools

import jax
import jax.numpy as jnp
from jax import lax
from jax.experimental import pallas as pl
from jax.experimental.pallas import tpu as pltpu
from jax.sharding import PartitionSpec as P

HIGH = lax.Precision.HIGHEST
F32 = jnp.float32
BF16 = jnp.bfloat16
LIMIT = 60 * 1024 * 1024


def dot(left, right, left_dim=1, right_dim=0, precision=HIGH):
    return lax.dot_general(
        left, right, (((left_dim,), (right_dim,)), ((), ())), precision=precision, preferred_element_type=F32
    )


def square(size):
    row = lax.broadcasted_iota(jnp.int32, (size, size), 0)
    return row, lax.broadcasted_iota(jnp.int32, (size, size), 1)


CHUNKS = 8
SIDE = 4


def mul(left, right):
    return jnp.dot(left, right, preferred_element_type=F32)


def front_kernel(
    where_ref, rows_hbm, sketch_hbm, sketched_hbm, piece_ref, piece_away_ref, away_send, away_keep, send, keep,
    rows, sketch, sketched, split, blocks, row_sems, sketch_sems, sketched_sem, away_sems, own_sems, *, scale,
):
    depth = rows.shape[1] // CHUNKS
    rank = sketched.shape[1]
    half, width = blocks.shape[2:]
    core = where_ref[0]
    copies = []
    for c in range(CHUNKS):
        part = pl.ds(c * depth, depth)
        pair = (
            pltpu.make_async_copy(sketch_hbm.at[part], sketch.at[part], sketch_sems.at[c]),
            pltpu.make_async_copy(rows_hbm.at[:, part], rows.at[:, part], row_sems.at[c]),
        )
        for copy in pair:
            copy.start()
        copies.append(pair)
    for c in range(CHUNKS):
        for copy in copies[c]:
            copy.wait()
        part = slice(c * depth, (c + 1) * depth)
        term = mul(rows[:, part], sketch[part, :])
        sketched[...] = term if c == 0 else sketched[...] + term
    sketched_copy = pltpu.make_async_copy(sketched, sketched_hbm, sketched_sem)
    sketched_copy.start()

    value = sketched[...]
    high = value.astype(BF16)
    rest = value - high.astype(F32)
    low = rest.astype(BF16)
    last = (rest - low.astype(F32)).astype(BF16)
    turned_high, turned_low = high.T, low.T
    split[:rank, :] = turned_high
    split[rank:, :] = turned_low
    even = mul(turned_high, high) + mul(turned_low, low)
    cross = mul(turned_high, low) + mul(turned_high, last)
    gram = (even + (cross + cross.T)) * scale
    row, col = square(half)
    end = gram[half:, half:]
    diagonal = jnp.sum(jnp.where(row == col, end, 0.0), axis=0, keepdims=True)
    corner = jnp.concatenate([gram[:half, half:], jnp.zeros((8, half), F32)])
    mixed = jnp.concatenate(
        [jnp.where(row <= col, gram[:half, :half], end), jnp.broadcast_to(diagonal, (8, half))]
    )
    piece_ref[...] = jnp.where(core == 0, corner, mixed)
    piece_away_ref[...] = jnp.where(core == 0, mixed, corner)

    outs = []
    for y in range(SIDE):
        for x in range(SIDE):
            slot = y * SIDE + x
            both = mul(split[...], rows[:, slot * width : (slot + 1) * width])
            both = both[:rank] + both[rank:]
            blocks[0, slot] = both[:half]
            blocks[1, slot] = both[half:]
            for which, bit, refs, sems in (
                (1 - core, where_ref[2], (away_send, away_keep), away_sems),
                (core, where_ref[1], (send, keep), own_sems),
            ):
                outer, inner = jnp.where(which == 0, x, y), jnp.where(which == 0, y, x)
                stays = outer % 2 == bit
                for ref, wanted in zip(refs, (jnp.logical_not(stays), stays)):
                    to = ref.at[outer // 2, inner]
                    copy = pltpu.make_async_copy(blocks.at[which, slot], to, sems.at[slot])
                    pl.when(wanted)(copy.start)
                    outs.append((wanted, copy))
    for wanted, copy in outs:
        pl.when(wanted)(copy.wait)
    sketched_copy.wait()


def front(where, embeddings, sketch, scale):
    count, width = embeddings.shape
    rank = sketch.shape[1]
    half = rank // 2
    hbm = pl.BlockSpec(memory_space=pl.ANY)
    vmem = pl.BlockSpec(memory_space=pltpu.VMEM)
    piece = jax.ShapeDtypeStruct((half + 8, half), F32)
    term = jax.ShapeDtypeStruct((SIDE // 2, SIDE, half, width // SIDE**2), F32)
    return pl.pallas_call(
        functools.partial(front_kernel, scale=scale),
        in_specs=[pl.BlockSpec(memory_space=pltpu.SMEM), hbm, hbm],
        out_specs=[hbm, vmem, vmem, hbm, hbm, hbm, hbm],
        out_shape=[jax.ShapeDtypeStruct((count, rank), F32), piece, piece, term, term, term, term],
        scratch_shapes=[
            pltpu.VMEM((count, width), BF16),
            pltpu.VMEM((width, rank), BF16),
            pltpu.VMEM((count, rank), F32),
            pltpu.VMEM((2 * rank, count), BF16),
            pltpu.VMEM((2, SIDE**2, half, width // SIDE**2), F32),
            pltpu.SemaphoreType.DMA((CHUNKS,)),
            pltpu.SemaphoreType.DMA((CHUNKS,)),
            pltpu.SemaphoreType.DMA,
            pltpu.SemaphoreType.DMA((SIDE**2,)),
            pltpu.SemaphoreType.DMA((SIDE**2,)),
        ],
        compiler_params=pltpu.CompilerParams(vmem_limit_bytes=LIMIT),
        cost_estimate=pl.CostEstimate(flops=6 * count * width * rank, bytes_accessed=2**24, transcendentals=0),
        name="front",
    )(where, embeddings, sketch)


def eliminate(pair, size):
    index = lax.broadcasted_iota(jnp.int32, (size, 1), 0)
    lanes = pair.shape[1]
    for j in range(0, size, 8):
        rows = [pair[j + p : j + p + 1, :] for p in range(8)]
        a = {
            (p, q): jnp.broadcast_to(rows[p][:, j + q : j + q + 1], (1, lanes))
            for p in range(8)
            for q in range(p, 8)
        }
        done, steps = [], []
        for s in range(0, 8, 2):
            aa, ab, bb = a[s, s], a[s, s + 1], a[s + 1, s + 1]
            inverse = 1.0 / (aa * bb - ab * ab)
            u, v = rows[s], rows[s + 1]
            top = (bb * u - ab * v) * inverse
            low = (aa * v - ab * u) * inverse
            done += [u, v - (ab / aa) * u]
            cross = {
                q: (
                    (bb * a[s, q] - ab * a[s + 1, q]) * inverse,
                    (aa * a[s + 1, q] - ab * a[s, q]) * inverse,
                )
                for q in range(s + 2, 8)
            }
            for p in range(s + 2, 8):
                rows[p] = rows[p] - (a[s, p] * top + a[s + 1, p] * low)
                for q in range(p, 8):
                    a[p, q] = a[p, q] - (a[s, p] * cross[q][0] + a[s + 1, p] * cross[q][1])
            steps.append((top, low, cross))
        weight = {}
        for s in (6, 4, 2, 0):
            top, low, cross = steps[s // 2]
            for q in range(s + 2, 8):
                top = top - cross[q][0] * weight[q]
                low = low - cross[q][1] * weight[q]
            weight[s], weight[s + 1] = top, low
        if j + 8 == size:
            return jnp.concatenate([pair[:j]] + done, axis=0)
        below = index > j + 7
        total = None
        for p in range(8):
            part = jnp.where(below, pair[:, j + p : j + p + 1], 0.0) * weight[p]
            total = part if total is None else total + part
        rest = pair - total
        pair = jnp.concatenate(([rest[:j]] if j else []) + done + [rest[j + 8 :]], axis=0)
    return pair


def step_blocks(work, upper_ref, blocks, block):
    size = work.shape[0]
    row, col = square(block)
    identity = (row == col).astype(F32)
    for k in blocks:
        lo, hi = k * block, (k + 1) * block
        pair = eliminate(jnp.concatenate([work[lo:hi, lo:hi], identity], axis=1), block)
        diagonal = jnp.sum(jnp.where(row == col, pair[:, :block], 0.0), axis=1, keepdims=True)
        pair = pair * (1.0 / jnp.sqrt(diagonal))
        small = pair[:, block:]
        upper_ref[lo:hi, :] = jnp.where(row <= col, pair[:, :block], 0.0)
        wide = dot(small, work[lo:hi, :])
        left = [wide[:, :lo]] if lo else []
        right = [wide[:, hi:]] if hi < size else []
        wide = jnp.concatenate(left + [small] + right, axis=1)
        if hi < size:
            tall = dot(work[hi:, lo:hi], small, 1, 1)
            lane = lax.broadcasted_iota(jnp.int32, (size - hi, size), 1)
            old = jnp.where((lane >= lo) & (lane < hi), 0.0, work[hi:, :])
            work[hi:, :] = old - dot(tall, wide)
        work[lo:hi, :] = wide


def first_kernel(corner_ref, mixed_ref, work, upper_ref, scales_ref, *, block):
    size = work.shape[0]
    half = size // 2
    row, col = square(half)
    eye = row == col
    corner, mixed = corner_ref[:half, :], mixed_ref[:half, :]
    turned = mixed.T
    first = jnp.where(row <= col, mixed, turned)
    last = jnp.where(eye, mixed_ref[half : half + 1, :], jnp.where(row > col, mixed, turned))

    def scales(matrix):
        picked = jnp.where(eye, matrix, 0.0)
        across = jnp.sqrt(jnp.sum(picked, axis=0, keepdims=True))
        down = jnp.sqrt(jnp.sum(picked, axis=1, keepdims=True))
        return across, 1.0 / across, 1.0 / down

    root_a, lane_a, sub_a = scales(first)
    root_b, lane_b, sub_b = scales(last)
    scales_ref[0:1, :] = jnp.concatenate([root_a, root_b], axis=1)
    scales_ref[1:2, :] = jnp.concatenate([lane_a, lane_b], axis=1)
    work[:half, :half] = jnp.where(eye, 1.0, first * sub_a * lane_a)
    work[half:, half:] = jnp.where(eye, 1.0, last * sub_b * lane_b)
    middle = corner * sub_a * lane_b
    work[:half, half:] = middle
    work[half:, :half] = middle.T
    step_blocks(work, upper_ref, range(half // block), block)


def second_kernel(state_ref, upper_ref, scales_ref, factor_ref, inverse_ref, work, upper, *, block):
    size = work.shape[0]
    half = size // 2
    work[...] = state_ref[...]
    upper[:half, :] = upper_ref[:half, :]
    step_blocks(work, upper, range(half // block, size // block), block)
    lane = lax.broadcasted_iota(jnp.int32, (block, size), 1)
    root, back = scales_ref[0:1, :], scales_ref[1:2, :]
    for k in range(size // block):
        lo, hi = k * block, (k + 1) * block
        value = work[lo:hi, :]
        inverse_ref[lo:hi, :] = jnp.where(lane < hi, value, 0.0) * back
        factor_ref[lo:hi, :] = jnp.where(lane >= hi, value, 0.0) * root
        factor_ref[lo:hi, lo:hi] = upper[lo:hi, :] * root[:, lo:hi]


SMALL = 12 * 1024 * 1024


def estimate(microseconds):
    return pl.CostEstimate(flops=microseconds * 2**30, bytes_accessed=2**20, transcendentals=0)


def factorize_first(corner, mixed, size, block):
    return pl.pallas_call(
        functools.partial(first_kernel, block=block),
        out_shape=[
            jax.ShapeDtypeStruct((size, size), F32),
            jax.ShapeDtypeStruct((size, block), F32),
            jax.ShapeDtypeStruct((8, size), F32),
        ],
        compiler_params=pltpu.CompilerParams(vmem_limit_bytes=SMALL),
        cost_estimate=estimate(6),
        name="factorize_first",
    )(corner, mixed)


def factorize_second(state, upper, scales, block):
    size = state.shape[0]
    return pl.pallas_call(
        functools.partial(second_kernel, block=block),
        out_shape=[jax.ShapeDtypeStruct((size, size), F32)] * 2,
        scratch_shapes=[pltpu.VMEM((size, size), F32), pltpu.VMEM((size, block), F32)],
        compiler_params=pltpu.CompilerParams(vmem_limit_bytes=SMALL),
        cost_estimate=estimate(6),
        name="factorize_second",
    )(state, upper, scales)


def basis_kernel(sketched_ref, inverse_ref, basis_ref):
    basis_ref[...] = dot(sketched_ref[...], inverse_ref[...], 1, 1).astype(BF16)


def basis_of(sketched, inverse):
    return pl.pallas_call(
        basis_kernel,
        out_shape=jax.ShapeDtypeStruct(sketched.shape, BF16),
        compiler_params=pltpu.CompilerParams(vmem_limit_bytes=SMALL),
        cost_estimate=estimate(2),
        name="basis",
    )(sketched, inverse)


def trade(value, masks):
    across, along = lax.axis_size("gx"), lax.axis_size("gy")
    pairs = []
    for i in range(across):
        mask_x, mask_y = masks[i % 2]
        for j in range(along):
            pairs.append((i * along + j, (i ^ mask_x) * along + (j ^ mask_y)))
    return lax.ppermute(value, ("gx", "gy"), pairs)


X1, X2, Y1, Y2 = (0, 1), (0, 2), (0, 4), (0, 8)
Z1, Z2, Z7 = (2, 0), (4, 0), (14, 0)
CORE = ((1, 0), (1, 0))


X3, Y3 = (0, 3), (0, 12)


def halves(value, bit, dim):
    keep = lax.dynamic_index_in_dim(value, bit, dim, keepdims=False)
    return keep, lax.dynamic_index_in_dim(value, 1 - bit, dim, keepdims=False)


def after(value, *others):
    return lax.optimization_barrier((value, *others))[0]


def order(core, mine, other):
    return jnp.where(core == 0, jnp.stack([mine, other]), jnp.stack([other, mine]))


def body(embeddings, sketch):
    total_rows = embeddings.shape[0] * lax.axis_size("gx") * lax.axis_size("gy")
    rank = sketch.shape[1]
    core = lax.axis_index("gx") % 2
    place = lax.axis_index("gy")
    x, y = place % SIDE, place // SIDE
    outer, inner = jnp.where(core == 0, x, y), jnp.where(core == 0, y, x)
    where = jnp.stack([core, outer % 2, inner % 2]).astype(jnp.int32)
    sketched, piece, piece_away, *terms = front(where, embeddings, sketch, 1.0 / total_rows)
    away_send, away_keep, send, keep = terms
    away_send = trade(away_send, CORE)
    away_keep = trade(away_keep, CORE)

    piece = piece + trade(piece_away, CORE)
    sums = [piece]
    for masks in ((Z1, Z7), (Z2, Z2), (Z7, Z1), (X1, Y1), (X3, Y3), (Y1, X1), (Y3, X3)):
        sums.append(sums[-1] + trade(sums[-1], masks))
    piece = sums[-1]
    other = trade(piece, CORE)
    corner, mixed = jnp.where(core == 0, piece, other), jnp.where(core == 0, other, piece)

    send = after(send + away_send, sums[0])
    got = jnp.stack([trade(send[0], (X1, Y1)), trade(send[1], (X3, Y3))])
    term = (keep + away_keep) + got
    half, width = term.shape[2:]
    keep, send = halves(term.reshape(2, 2, 2, half, width), inner % 2, 2)
    term = keep + trade(after(send, sums[2]), (Y1, X1))
    keep, send = halves(term, outer // 2, 0)
    term = keep + trade(after(send, sums[4]), (X2, Y2))
    keep, send = halves(term, inner // 2, 0)
    term = keep + trade(after(send, sums[6]), (Y2, X2))
    term = after(term, sums[7])
    term = term + trade(term, (Z1, Z7))
    block = 64
    state = factorize_first(corner, mixed, rank, block)
    state = after(tuple(state), term)
    term = term + trade(term, (Z2, Z2))
    factor, inverse = factorize_second(*state, block)
    factor, inverse = after((factor, inverse), term)
    term = term + trade(term, (Z7, Z1))
    basis = basis_of(sketched, inverse)
    summed = order(core, term, trade(term, CORE)).reshape(rank, width)

    row_count = rank // lax.axis_size("gx")
    mine = lax.dynamic_slice_in_dim(inverse, lax.axis_index("gx") * row_count, row_count, 0)
    projection = dot(mine, summed) / total_rows
    return (basis, factor, projection)


def solution(mesh):
    placed = (P(("gx", "gy"), None), P())
    return jax.shard_map(
        body,
        mesh=mesh,
        in_specs=placed,
        out_specs=(P(("gx", "gy"), None), P(), P("gx", "gy")),
        check_vma=False,
    )
```

```python
import functools

import jax
import jax.numpy as jnp
from jax import lax
from jax.experimental import pallas as pl
from jax.experimental.pallas import tpu as pltpu
from jax.sharding import PartitionSpec as P

HIGH = lax.Precision.HIGHEST
F32 = jnp.float32
BF16 = jnp.bfloat16
LIMIT = 60 * 1024 * 1024


def dot(left, right, left_dim=1, right_dim=0, precision=HIGH):
    return lax.dot_general(
        left, right, (((left_dim,), (right_dim,)), ((), ())), precision=precision, preferred_element_type=F32
    )


def square(size):
    row = lax.broadcasted_iota(jnp.int32, (size, size), 0)
    return row, lax.broadcasted_iota(jnp.int32, (size, size), 1)


CHUNKS = 8
SIDE = 4


def mul(left, right):
    return jnp.dot(left, right, preferred_element_type=F32)


def front_kernel(
    where_ref, rows_hbm, sketch_hbm, sketched_hbm, piece_ref, piece_away_ref, away_send, away_keep, send, keep,
    rows, sketch, sketched, split, blocks, row_sems, sketch_sems, sketched_sem, away_sems, own_sems, *, scale,
):
    depth = rows.shape[1] // CHUNKS
    rank = sketched.shape[1]
    half, width = blocks.shape[2:]
    core = where_ref[0]
    copies = []
    for c in range(CHUNKS):
        part = pl.ds(c * depth, depth)
        pair = (
            pltpu.make_async_copy(sketch_hbm.at[part], sketch.at[part], sketch_sems.at[c]),
            pltpu.make_async_copy(rows_hbm.at[:, part], rows.at[:, part], row_sems.at[c]),
        )
        for copy in pair:
            copy.start()
        copies.append(pair)
    for c in range(CHUNKS):
        for copy in copies[c]:
            copy.wait()
        part = slice(c * depth, (c + 1) * depth)
        term = mul(rows[:, part], sketch[part, :])
        sketched[...] = term if c == 0 else sketched[...] + term
    sketched_copy = pltpu.make_async_copy(sketched, sketched_hbm, sketched_sem)
    sketched_copy.start()

    value = sketched[...]
    high = value.astype(BF16)
    rest = value - high.astype(F32)
    low = rest.astype(BF16)
    last = (rest - low.astype(F32)).astype(BF16)
    turned_high, turned_low = high.T, low.T
    split[:rank, :] = turned_high
    split[rank:, :] = turned_low
    even = mul(turned_high, high) + mul(turned_low, low)
    cross = mul(turned_high, low) + mul(turned_high, last)
    gram = (even + (cross + cross.T)) * scale
    row, col = square(half)
    end = gram[half:, half:]
    diagonal = jnp.sum(jnp.where(row == col, end, 0.0), axis=0, keepdims=True)
    corner, mixed = gram[:half, half:], jnp.where(row <= col, gram[:half, :half], end)
    upper = half // 2
    for ref, first in ((piece_ref, core == 0), (piece_away_ref, core == 1)):
        value = jnp.where(first, corner, mixed)
        ref[:upper, :half] = value[:upper]
        ref[:upper, half:] = value[upper:]
        ref[upper:, :] = jnp.broadcast_to(jnp.concatenate([diagonal, diagonal], axis=1), (8, rank))

    outs = []
    for y in range(SIDE):
        for x in range(SIDE):
            slot = y * SIDE + x
            both = mul(split[...], rows[:, slot * width : (slot + 1) * width])
            both = both[:rank] + both[rank:]
            blocks[0, slot] = both[:half]
            blocks[1, slot] = both[half:]
            for which, bit, refs, sems in (
                (1 - core, where_ref[2], (away_send, away_keep), away_sems),
                (core, where_ref[1], (send, keep), own_sems),
            ):
                outer, inner = jnp.where(which == 0, x, y), jnp.where(which == 0, y, x)
                stays = outer % 2 == bit
                for ref, wanted in zip(refs, (jnp.logical_not(stays), stays)):
                    to = ref.at[outer // 2, inner]
                    copy = pltpu.make_async_copy(blocks.at[which, slot], to, sems.at[slot])
                    pl.when(wanted)(copy.start)
                    outs.append((wanted, copy))
    for wanted, copy in outs:
        pl.when(wanted)(copy.wait)
    sketched_copy.wait()


def front(where, embeddings, sketch, scale):
    count, width = embeddings.shape
    rank = sketch.shape[1]
    half = rank // 2
    hbm = pl.BlockSpec(memory_space=pl.ANY)
    vmem = pl.BlockSpec(memory_space=pltpu.VMEM)
    piece = jax.ShapeDtypeStruct((half // 2 + 8, rank), F32)
    term = jax.ShapeDtypeStruct((SIDE // 2, SIDE, half, width // SIDE**2), F32)
    return pl.pallas_call(
        functools.partial(front_kernel, scale=scale),
        in_specs=[pl.BlockSpec(memory_space=pltpu.SMEM), hbm, hbm],
        out_specs=[hbm, vmem, vmem, hbm, hbm, hbm, hbm],
        out_shape=[jax.ShapeDtypeStruct((count, rank), F32), piece, piece, term, term, term, term],
        scratch_shapes=[
            pltpu.VMEM((count, width), BF16),
            pltpu.VMEM((width, rank), BF16),
            pltpu.VMEM((count, rank), F32),
            pltpu.VMEM((2 * rank, count), BF16),
            pltpu.VMEM((2, SIDE**2, half, width // SIDE**2), F32),
            pltpu.SemaphoreType.DMA((CHUNKS,)),
            pltpu.SemaphoreType.DMA((CHUNKS,)),
            pltpu.SemaphoreType.DMA,
            pltpu.SemaphoreType.DMA((SIDE**2,)),
            pltpu.SemaphoreType.DMA((SIDE**2,)),
        ],
        compiler_params=pltpu.CompilerParams(vmem_limit_bytes=LIMIT),
        cost_estimate=pl.CostEstimate(flops=6 * count * width * rank, bytes_accessed=2**24, transcendentals=0),
        name="front",
    )(where, embeddings, sketch)


def eliminate(pair, size):
    index = lax.broadcasted_iota(jnp.int32, (size, 1), 0)
    lanes = pair.shape[1]
    for j in range(0, size, 8):
        rows = [pair[j + p : j + p + 1, :] for p in range(8)]
        a = {
            (p, q): jnp.broadcast_to(rows[p][:, j + q : j + q + 1], (1, lanes))
            for p in range(8)
            for q in range(p, 8)
        }
        done, steps = [], []
        for s in range(0, 8, 2):
            aa, ab, bb = a[s, s], a[s, s + 1], a[s + 1, s + 1]
            inverse = 1.0 / (aa * bb - ab * ab)
            u, v = rows[s], rows[s + 1]
            top = (bb * u - ab * v) * inverse
            low = (aa * v - ab * u) * inverse
            done += [u, v - (ab / aa) * u]
            cross = {
                q: (
                    (bb * a[s, q] - ab * a[s + 1, q]) * inverse,
                    (aa * a[s + 1, q] - ab * a[s, q]) * inverse,
                )
                for q in range(s + 2, 8)
            }
            for p in range(s + 2, 8):
                rows[p] = rows[p] - (a[s, p] * top + a[s + 1, p] * low)
                for q in range(p, 8):
                    a[p, q] = a[p, q] - (a[s, p] * cross[q][0] + a[s + 1, p] * cross[q][1])
            steps.append((top, low, cross))
        weight = {}
        for s in (6, 4, 2, 0):
            top, low, cross = steps[s // 2]
            for q in range(s + 2, 8):
                top = top - cross[q][0] * weight[q]
                low = low - cross[q][1] * weight[q]
            weight[s], weight[s + 1] = top, low
        if j + 8 == size:
            return jnp.concatenate([pair[:j]] + done, axis=0)
        below = index > j + 7
        total = None
        for p in range(8):
            part = jnp.where(below, pair[:, j + p : j + p + 1], 0.0) * weight[p]
            total = part if total is None else total + part
        rest = pair - total
        pair = jnp.concatenate(([rest[:j]] if j else []) + done + [rest[j + 8 :]], axis=0)
    return pair


def step_blocks(work, upper_ref, blocks, block):
    size = work.shape[0]
    row, col = square(block)
    identity = (row == col).astype(F32)
    for k in blocks:
        lo, hi = k * block, (k + 1) * block
        pair = eliminate(jnp.concatenate([work[lo:hi, lo:hi], identity], axis=1), block)
        diagonal = jnp.sum(jnp.where(row == col, pair[:, :block], 0.0), axis=1, keepdims=True)
        pair = pair * (1.0 / jnp.sqrt(diagonal))
        small = pair[:, block:]
        upper_ref[lo:hi, :] = jnp.where(row <= col, pair[:, :block], 0.0)
        wide = dot(small, work[lo:hi, :])
        left = [wide[:, :lo]] if lo else []
        right = [wide[:, hi:]] if hi < size else []
        wide = jnp.concatenate(left + [small] + right, axis=1)
        if hi < size:
            tall = dot(work[hi:, lo:hi], small, 1, 1)
            lane = lax.broadcasted_iota(jnp.int32, (size - hi, size), 1)
            old = jnp.where((lane >= lo) & (lane < hi), 0.0, work[hi:, :])
            work[hi:, :] = old - dot(tall, wide)
        work[lo:hi, :] = wide


def first_kernel(corner_ref, mixed_ref, work, upper_ref, scales_ref, *, block):
    size = work.shape[0]
    half = size // 2
    row, col = square(half)
    eye = row == col
    upper = half // 2
    corner, mixed = (
        jnp.concatenate([ref[:upper, :half], ref[:upper, half:]]) for ref in (corner_ref, mixed_ref)
    )
    turned = mixed.T
    first = jnp.where(row <= col, mixed, turned)
    last = jnp.where(eye, mixed_ref[upper : upper + 1, :half], jnp.where(row > col, mixed, turned))

    def scales(matrix):
        picked = jnp.where(eye, matrix, 0.0)
        across = jnp.sqrt(jnp.sum(picked, axis=0, keepdims=True))
        down = jnp.sqrt(jnp.sum(picked, axis=1, keepdims=True))
        return across, 1.0 / across, 1.0 / down

    root_a, lane_a, sub_a = scales(first)
    root_b, lane_b, sub_b = scales(last)
    scales_ref[0:1, :] = jnp.concatenate([root_a, root_b], axis=1)
    scales_ref[1:2, :] = jnp.concatenate([lane_a, lane_b], axis=1)
    work[:half, :half] = jnp.where(eye, 1.0, first * sub_a * lane_a)
    work[half:, half:] = jnp.where(eye, 1.0, last * sub_b * lane_b)
    middle = corner * sub_a * lane_b
    work[:half, half:] = middle
    work[half:, :half] = middle.T
    step_blocks(work, upper_ref, range(half // block), block)


def second_kernel(state_ref, upper_ref, scales_ref, factor_ref, inverse_ref, work, upper, *, block):
    size = work.shape[0]
    half = size // 2
    work[...] = state_ref[...]
    upper[:half, :] = upper_ref[:half, :]
    step_blocks(work, upper, range(half // block, size // block), block)
    lane = lax.broadcasted_iota(jnp.int32, (block, size), 1)
    root, back = scales_ref[0:1, :], scales_ref[1:2, :]
    for k in range(size // block):
        lo, hi = k * block, (k + 1) * block
        value = work[lo:hi, :]
        inverse_ref[lo:hi, :] = jnp.where(lane < hi, value, 0.0) * back
        factor_ref[lo:hi, :] = jnp.where(lane >= hi, value, 0.0) * root
        factor_ref[lo:hi, lo:hi] = upper[lo:hi, :] * root[:, lo:hi]


SMALL = 12 * 1024 * 1024


def estimate(microseconds):
    return pl.CostEstimate(flops=microseconds * 2**30, bytes_accessed=2**20, transcendentals=0)


def factorize_first(corner, mixed, size, block):
    return pl.pallas_call(
        functools.partial(first_kernel, block=block),
        out_shape=[
            jax.ShapeDtypeStruct((size, size), F32),
            jax.ShapeDtypeStruct((size, block), F32),
            jax.ShapeDtypeStruct((8, size), F32),
        ],
        compiler_params=pltpu.CompilerParams(vmem_limit_bytes=SMALL),
        cost_estimate=estimate(6),
        name="factorize_first",
    )(corner, mixed)


def factorize_second(state, upper, scales, block):
    size = state.shape[0]
    return pl.pallas_call(
        functools.partial(second_kernel, block=block),
        out_shape=[jax.ShapeDtypeStruct((size, size), F32)] * 2,
        scratch_shapes=[pltpu.VMEM((size, size), F32), pltpu.VMEM((size, block), F32)],
        compiler_params=pltpu.CompilerParams(vmem_limit_bytes=SMALL),
        cost_estimate=estimate(6),
        name="factorize_second",
    )(state, upper, scales)


def basis_kernel(sketched_ref, inverse_ref, basis_ref):
    basis_ref[...] = dot(sketched_ref[...], inverse_ref[...], 1, 1).astype(BF16)


def basis_of(sketched, inverse):
    return pl.pallas_call(
        basis_kernel,
        out_shape=jax.ShapeDtypeStruct(sketched.shape, BF16),
        compiler_params=pltpu.CompilerParams(vmem_limit_bytes=SMALL),
        cost_estimate=estimate(2),
        name="basis",
    )(sketched, inverse)


def trade(value, masks):
    across, along = lax.axis_size("gx"), lax.axis_size("gy")
    pairs = []
    for i in range(across):
        mask_x, mask_y = masks[i % 2]
        for j in range(along):
            pairs.append((i * along + j, (i ^ mask_x) * along + (j ^ mask_y)))
    return lax.ppermute(value, ("gx", "gy"), pairs)


X1, X2, Y1, Y2 = (0, 1), (0, 2), (0, 4), (0, 8)
Z1, Z2, Z7 = (2, 0), (4, 0), (14, 0)
CORE = ((1, 0), (1, 0))


X3, Y3, XY2 = (0, 3), (0, 12), (0, 10)


def halves(value, bit, dim):
    keep = lax.dynamic_index_in_dim(value, bit, dim, keepdims=False)
    return keep, lax.dynamic_index_in_dim(value, 1 - bit, dim, keepdims=False)


def trade_both(value, piece, masks):
    flat = value.reshape(-1, piece.shape[1])
    got = trade(jnp.concatenate([flat, piece]), masks)
    return got[: flat.shape[0]].reshape(value.shape), got[flat.shape[0] :]


def after(value, *others):
    return lax.optimization_barrier((value, *others))[0]


def order(core, mine, other):
    return jnp.where(core == 0, jnp.stack([mine, other]), jnp.stack([other, mine]))


def body(embeddings, sketch):
    total_rows = embeddings.shape[0] * lax.axis_size("gx") * lax.axis_size("gy")
    rank = sketch.shape[1]
    core = lax.axis_index("gx") % 2
    place = lax.axis_index("gy")
    x, y = place % SIDE, place // SIDE
    outer, inner = jnp.where(core == 0, x, y), jnp.where(core == 0, y, x)
    where = jnp.stack([core, outer % 2, inner % 2]).astype(jnp.int32)
    sketched, piece, piece_away, *terms = front(where, embeddings, sketch, 1.0 / total_rows)
    away_send, away_keep, send, keep = terms
    half, width = keep.shape[2:]

    piece = piece + trade(piece_away, CORE)
    send = send + trade(away_send, CORE)
    keep = keep + trade(after(away_keep, piece), CORE)
    one, piece_1 = trade_both(send[0], piece, (X1, Y1))
    three, piece_3 = trade_both(send[1], piece, (X3, Y3))
    piece = (piece + piece_1) + (trade(piece, (X2, Y2)) + piece_3)
    terms = [(k + got).reshape(2, 2, half, width) for k, got in zip(keep, (one, three))]
    parts = [halves(term, inner % 2, 1) for term in terms]
    one, piece_1 = trade_both(parts[0][1], piece, (Y1, X1))
    three, piece_3 = trade_both(parts[1][1], piece, (Y3, X3))
    piece = (piece + piece_1) + (trade(piece, (Y2, X2)) + piece_3)
    low, high = (part[0] + got for part, got in zip(parts, (one, three)))
    outer, inner = outer // 2, inner // 2

    def quarter(across, along):
        pair = jnp.where((outer ^ across) == 1, high, low)
        return lax.dynamic_index_in_dim(pair, inner ^ along, 0, keepdims=False)

    one = trade(quarter(1, 1), (XY2, XY2))
    two = trade(quarter(1, 0), (X2, Y2))
    three = trade(quarter(0, 1), (Y2, X2))
    piece = piece + trade(piece, (Z7, Z7))
    term = (quarter(0, 0) + one) + (two + three)
    piece = piece + trade(piece, (Z2, Z1))
    piece = piece + trade(piece, (Z1, Z2))

    other = trade(piece, CORE)
    corner, mixed = jnp.where(core == 0, piece, other), jnp.where(core == 0, other, piece)
    block = 64
    term = term + trade(term, (Z1, Z2))
    term, corner, mixed = lax.optimization_barrier((term, corner, mixed))
    state = factorize_first(corner, mixed, rank, block)
    term = term + trade(term, (Z2, Z1))
    term, *state = lax.optimization_barrier((term, *state))
    factor, inverse = factorize_second(*state, block)
    term = term + trade(term, (Z7, Z7))
    term, factor, inverse = lax.optimization_barrier((term, factor, inverse))
    basis = basis_of(sketched, inverse)
    summed = order(core, term, trade(term, CORE)).reshape(rank, width)

    row_count = rank // lax.axis_size("gx")
    mine = lax.dynamic_slice_in_dim(inverse, lax.axis_index("gx") * row_count, row_count, 0)
    projection = dot(mine, summed) / total_rows
    return (basis, factor, projection)


def solution(mesh):
    placed = (P(("gx", "gy"), None), P())
    return jax.shard_map(
        body,
        mesh=mesh,
        in_specs=placed,
        out_specs=(P(("gx", "gy"), None), P(), P("gx", "gy")),
        check_vma=False,
    )
```

```python
import functools

import jax
import jax.numpy as jnp
from jax import lax
from jax.experimental import pallas as pl
from jax.experimental.pallas import tpu as pltpu
from jax.sharding import PartitionSpec as P

HIGH = lax.Precision.HIGHEST
F32 = jnp.float32
BF16 = jnp.bfloat16
LIMIT = 60 * 1024 * 1024


def dot(left, right, left_dim=1, right_dim=0, precision=HIGH):
    return lax.dot_general(
        left, right, (((left_dim,), (right_dim,)), ((), ())), precision=precision, preferred_element_type=F32
    )


def square(size):
    row = lax.broadcasted_iota(jnp.int32, (size, size), 0)
    return row, lax.broadcasted_iota(jnp.int32, (size, size), 1)


CHUNKS = 8
SIDE = 4


def mul(left, right):
    return jnp.dot(left, right, preferred_element_type=F32)


def position():
    core, place = lax.axis_index("gx") % 2, lax.axis_index("gy")
    x, y = place % SIDE, place // SIDE
    return core, jnp.where(core == 0, x, y), jnp.where(core == 0, y, x)


def front_kernel(
    rows_hbm, sketch_hbm, sketched_hbm, away_send, away_keep, send, keep,
    rows, sketch, sketched, split, blocks, pieces, row_sems, sketch_sems, sketched_sem, away_sems, own_sems, piece_sems,
    *, scale,
):
    depth = rows.shape[1] // CHUNKS
    rank = sketched.shape[1]
    half, width = blocks.shape[2:]
    core, outer_place, inner_place = position()
    copies = []
    for c in range(CHUNKS):
        part = pl.ds(c * depth, depth)
        pair = (
            pltpu.make_async_copy(sketch_hbm.at[part], sketch.at[part], sketch_sems.at[c]),
            pltpu.make_async_copy(rows_hbm.at[:, part], rows.at[:, part], row_sems.at[c]),
        )
        for copy in pair:
            copy.start()
        copies.append(pair)
    for c in range(CHUNKS):
        for copy in copies[c]:
            copy.wait()
        part = slice(c * depth, (c + 1) * depth)
        term = mul(rows[:, part], sketch[part, :])
        sketched[...] = term if c == 0 else sketched[...] + term
    sketched_copy = pltpu.make_async_copy(sketched, sketched_hbm, sketched_sem)
    sketched_copy.start()

    value = sketched[...]
    high = value.astype(BF16)
    rest = value - high.astype(F32)
    low = rest.astype(BF16)
    last = (rest - low.astype(F32)).astype(BF16)
    turned_high, turned_low = high.T, low.T
    split[:rank, :] = turned_high
    split[rank:, :] = turned_low
    even = mul(turned_high, high) + mul(turned_low, low)
    cross = mul(turned_high, low) + mul(turned_high, last)
    gram = (even + (cross + cross.T)) * scale
    row, col = square(half)
    end = gram[half:, half:]
    diagonal = jnp.sum(jnp.where(row == col, end, 0.0), axis=0, keepdims=True)
    corner, mixed = gram[:half, half:], jnp.where(row <= col, gram[:half, :half], end)
    upper = half // 2
    for at, first in ((0, core == 0), (1, core == 1)):
        value = jnp.where(first, corner, mixed)
        pieces[at, :upper, :half] = value[:upper]
        pieces[at, :upper, half:] = value[upper:]
        pieces[at, upper:, :] = jnp.broadcast_to(jnp.concatenate([diagonal, diagonal], axis=1), (8, rank))
    pieces[2] = jnp.zeros_like(pieces[2])
    tail = pl.ds(SIDE * half, pieces.shape[1])
    tails = []
    for at, ref, side in (
        (0, send, 0), (0, send, 1), (0, keep, 0), (2, keep, 1),
        (1, away_send, 0), (1, away_send, 1), (1, away_keep, 0), (2, away_keep, 1),
    ):
        tails.append(pltpu.make_async_copy(pieces.at[at], ref.at[side, tail], piece_sems.at[len(tails)]))
        tails[-1].start()

    outs = []
    for y in range(SIDE):
        for x in range(SIDE):
            slot = y * SIDE + x
            both = mul(split[...], rows[:, slot * width : (slot + 1) * width])
            both = both[:rank] + both[rank:]
            blocks[0, slot] = both[:half]
            blocks[1, slot] = both[half:]
            for which, bit, refs, sems in (
                (1 - core, inner_place % 2, (away_send, away_keep), away_sems),
                (core, outer_place % 2, (send, keep), own_sems),
            ):
                outer, inner = jnp.where(which == 0, x, y), jnp.where(which == 0, y, x)
                stays = outer % 2 == bit
                for ref, wanted in zip(refs, (jnp.logical_not(stays), stays)):
                    to = ref.at[outer // 2, pl.ds(pl.multiple_of(inner * half, half), half)]
                    copy = pltpu.make_async_copy(blocks.at[which, slot], to, sems.at[slot])
                    pl.when(wanted)(copy.start)
                    outs.append((wanted, copy))
    for wanted, copy in outs:
        pl.when(wanted)(copy.wait)
    sketched_copy.wait()
    for copy in tails:
        copy.wait()


def front(embeddings, sketch, scale):
    count, width = embeddings.shape
    rank = sketch.shape[1]
    half = rank // 2
    hbm = pl.BlockSpec(memory_space=pl.ANY)
    piece = half // 2 + 8
    term = jax.ShapeDtypeStruct((SIDE // 2, SIDE * half + piece, rank), F32)
    return pl.pallas_call(
        functools.partial(front_kernel, scale=scale),
        in_specs=[hbm, hbm],
        out_specs=[hbm] * 5,
        out_shape=[jax.ShapeDtypeStruct((count, rank), F32), term, term, term, term],
        scratch_shapes=[
            pltpu.VMEM((count, width), BF16),
            pltpu.VMEM((width, rank), BF16),
            pltpu.VMEM((count, rank), F32),
            pltpu.VMEM((2 * rank, count), BF16),
            pltpu.VMEM((2, SIDE**2, half, width // SIDE**2), F32),
            pltpu.VMEM((3, piece, rank), F32),
            pltpu.SemaphoreType.DMA((CHUNKS,)),
            pltpu.SemaphoreType.DMA((CHUNKS,)),
            pltpu.SemaphoreType.DMA,
            pltpu.SemaphoreType.DMA((SIDE**2,)),
            pltpu.SemaphoreType.DMA((SIDE**2,)),
            pltpu.SemaphoreType.DMA((8,)),
        ],
        compiler_params=pltpu.CompilerParams(vmem_limit_bytes=LIMIT),
        cost_estimate=pl.CostEstimate(flops=6 * count * width * rank, bytes_accessed=2**24, transcendentals=0),
        name="front",
    )(embeddings, sketch)


def eliminate(pair, size):
    index = lax.broadcasted_iota(jnp.int32, (size, 1), 0)
    lanes = pair.shape[1]
    for j in range(0, size, 8):
        rows = [pair[j + p : j + p + 1, :] for p in range(8)]
        a = {
            (p, q): jnp.broadcast_to(rows[p][:, j + q : j + q + 1], (1, lanes))
            for p in range(8)
            for q in range(p, 8)
        }
        done, steps = [], []
        for s in range(0, 8, 2):
            aa, ab, bb = a[s, s], a[s, s + 1], a[s + 1, s + 1]
            inverse = 1.0 / (aa * bb - ab * ab)
            u, v = rows[s], rows[s + 1]
            top = (bb * u - ab * v) * inverse
            low = (aa * v - ab * u) * inverse
            done += [u, v - (ab / aa) * u]
            cross = {
                q: (
                    (bb * a[s, q] - ab * a[s + 1, q]) * inverse,
                    (aa * a[s + 1, q] - ab * a[s, q]) * inverse,
                )
                for q in range(s + 2, 8)
            }
            for p in range(s + 2, 8):
                rows[p] = rows[p] - (a[s, p] * top + a[s + 1, p] * low)
                for q in range(p, 8):
                    a[p, q] = a[p, q] - (a[s, p] * cross[q][0] + a[s + 1, p] * cross[q][1])
            steps.append((top, low, cross))
        weight = {}
        for s in (6, 4, 2, 0):
            top, low, cross = steps[s // 2]
            for q in range(s + 2, 8):
                top = top - cross[q][0] * weight[q]
                low = low - cross[q][1] * weight[q]
            weight[s], weight[s + 1] = top, low
        if j + 8 == size:
            return jnp.concatenate([pair[:j]] + done, axis=0)
        below = index > j + 7
        total = None
        for p in range(8):
            part = jnp.where(below, pair[:, j + p : j + p + 1], 0.0) * weight[p]
            total = part if total is None else total + part
        rest = pair - total
        pair = jnp.concatenate(([rest[:j]] if j else []) + done + [rest[j + 8 :]], axis=0)
    return pair


def step_blocks(work, upper_ref, blocks, block):
    size = work.shape[0]
    row, col = square(block)
    identity = (row == col).astype(F32)
    for k in blocks:
        lo, hi = k * block, (k + 1) * block
        pair = eliminate(jnp.concatenate([work[lo:hi, lo:hi], identity], axis=1), block)
        diagonal = jnp.sum(jnp.where(row == col, pair[:, :block], 0.0), axis=1, keepdims=True)
        pair = pair * (1.0 / jnp.sqrt(diagonal))
        small = pair[:, block:]
        upper_ref[lo:hi, :] = jnp.where(row <= col, pair[:, :block], 0.0)
        wide = dot(small, work[lo:hi, :])
        left = [wide[:, :lo]] if lo else []
        right = [wide[:, hi:]] if hi < size else []
        wide = jnp.concatenate(left + [small] + right, axis=1)
        if hi < size:
            tall = dot(work[hi:, lo:hi], small, 1, 1)
            lane = lax.broadcasted_iota(jnp.int32, (size - hi, size), 1)
            old = jnp.where((lane >= lo) & (lane < hi), 0.0, work[hi:, :])
            work[hi:, :] = old - dot(tall, wide)
        work[lo:hi, :] = wide


def first_kernel(corner_ref, mixed_ref, work, upper_ref, scales_ref, *, block):
    size = work.shape[0]
    half = size // 2
    row, col = square(half)
    eye = row == col
    upper = half // 2
    corner, mixed = (
        jnp.concatenate([ref[:upper, :half], ref[:upper, half:]]) for ref in (corner_ref, mixed_ref)
    )
    turned = mixed.T
    first = jnp.where(row <= col, mixed, turned)
    last = jnp.where(eye, mixed_ref[upper : upper + 1, :half], jnp.where(row > col, mixed, turned))

    def scales(matrix):
        picked = jnp.where(eye, matrix, 0.0)
        across = jnp.sqrt(jnp.sum(picked, axis=0, keepdims=True))
        down = jnp.sqrt(jnp.sum(picked, axis=1, keepdims=True))
        return across, 1.0 / across, 1.0 / down

    root_a, lane_a, sub_a = scales(first)
    root_b, lane_b, sub_b = scales(last)
    scales_ref[0:1, :] = jnp.concatenate([root_a, root_b], axis=1)
    scales_ref[1:2, :] = jnp.concatenate([lane_a, lane_b], axis=1)
    work[:half, :half] = jnp.where(eye, 1.0, first * sub_a * lane_a)
    work[half:, half:] = jnp.where(eye, 1.0, last * sub_b * lane_b)
    middle = corner * sub_a * lane_b
    work[:half, half:] = middle
    work[half:, :half] = middle.T
    step_blocks(work, upper_ref, range(half // block), block)


def second_kernel(state_ref, upper_ref, scales_ref, factor_ref, inverse_ref, work, upper, *, block):
    size = work.shape[0]
    half = size // 2
    work[...] = state_ref[...]
    upper[:half, :] = upper_ref[:half, :]
    step_blocks(work, upper, range(half // block, size // block), block)
    lane = lax.broadcasted_iota(jnp.int32, (block, size), 1)
    root, back = scales_ref[0:1, :], scales_ref[1:2, :]
    for k in range(size // block):
        lo, hi = k * block, (k + 1) * block
        value = work[lo:hi, :]
        inverse_ref[lo:hi, :] = jnp.where(lane < hi, value, 0.0) * back
        factor_ref[lo:hi, :] = jnp.where(lane >= hi, value, 0.0) * root
        factor_ref[lo:hi, lo:hi] = upper[lo:hi, :] * root[:, lo:hi]


SMALL = 12 * 1024 * 1024


def estimate(microseconds):
    return pl.CostEstimate(flops=microseconds * 2**30, bytes_accessed=2**20, transcendentals=0)


def factorize_first(corner, mixed, size, block):
    return pl.pallas_call(
        functools.partial(first_kernel, block=block),
        out_shape=[
            jax.ShapeDtypeStruct((size, size), F32),
            jax.ShapeDtypeStruct((size, block), F32),
            jax.ShapeDtypeStruct((8, size), F32),
        ],
        compiler_params=pltpu.CompilerParams(vmem_limit_bytes=SMALL),
        cost_estimate=estimate(6),
        name="factorize_first",
    )(corner, mixed)


def factorize_second(state, upper, scales, block):
    size = state.shape[0]
    return pl.pallas_call(
        functools.partial(second_kernel, block=block),
        out_shape=[jax.ShapeDtypeStruct((size, size), F32)] * 2,
        scratch_shapes=[pltpu.VMEM((size, size), F32), pltpu.VMEM((size, block), F32)],
        compiler_params=pltpu.CompilerParams(vmem_limit_bytes=SMALL),
        cost_estimate=estimate(6),
        name="factorize_second",
    )(state, upper, scales)


def basis_kernel(sketched_ref, inverse_ref, basis_ref):
    basis_ref[...] = dot(sketched_ref[...], inverse_ref[...], 1, 1).astype(BF16)


def basis_of(sketched, inverse):
    return pl.pallas_call(
        basis_kernel,
        out_shape=jax.ShapeDtypeStruct(sketched.shape, BF16),
        compiler_params=pltpu.CompilerParams(vmem_limit_bytes=SMALL),
        cost_estimate=estimate(2),
        name="basis",
    )(sketched, inverse)


def trade(value, masks):
    across, along = lax.axis_size("gx"), lax.axis_size("gy")
    pairs = []
    for i in range(across):
        mask_x, mask_y = masks[i % 2]
        for j in range(along):
            pairs.append((i * along + j, (i ^ mask_x) * along + (j ^ mask_y)))
    return lax.ppermute(value, ("gx", "gy"), pairs)


X1, X2, Y1, Y2 = (0, 1), (0, 2), (0, 4), (0, 8)
Z1, Z2, Z7 = (2, 0), (4, 0), (14, 0)
CORE = ((1, 0), (1, 0))


X3, Y3 = (0, 3), (0, 12)


def halves(value, bit, dim):
    keep = lax.dynamic_index_in_dim(value, bit, dim, keepdims=False)
    return keep, lax.dynamic_index_in_dim(value, 1 - bit, dim, keepdims=False)


def trade_both(value, piece, masks):
    flat = value.reshape(-1, piece.shape[1])
    got = trade(jnp.concatenate([flat, piece]), masks)
    return got[: flat.shape[0]].reshape(value.shape), got[flat.shape[0] :]


def after(value, *others):
    return lax.optimization_barrier((value, *others))[0]


def order(core, mine, other):
    return jnp.where(core == 0, jnp.stack([mine, other]), jnp.stack([other, mine]))


def body(embeddings, sketch):
    total_rows = embeddings.shape[0] * lax.axis_size("gx") * lax.axis_size("gy")
    rank = sketch.shape[1]
    core, outer, inner = position()
    sketched, away_send, away_keep, send, keep = front(embeddings, sketch, 1.0 / total_rows)
    half = rank // 2
    rows = SIDE * half

    message = send + trade(away_send, CORE)
    keep = keep + trade(after(away_keep, message), CORE)
    one = keep[0] + trade(message[0], (X1, Y1))
    three = keep[1] + trade(message[1], (X3, Y3))
    piece = one[rows:] + (trade(message[0, rows:], (X2, Y2)) + three[rows:])
    terms = [part[:rows].reshape(2, 2, half, -1) for part in (one, three)]
    parts = [halves(term, inner % 2, 1) for term in terms]
    one, piece_1 = trade_both(parts[0][1], piece, (Y1, X1))
    three, piece_3 = trade_both(parts[1][1], piece, (Y3, X3))
    piece = (piece + piece_1) + (trade(piece, (Y2, X2)) + piece_3)
    low, high = (part[0] + got for part, got in zip(parts, (one, three)))
    upper = outer // 2 == 1
    term = jnp.where(upper, high, low) + trade(jnp.where(upper, low, high), (X2, Y2))
    piece = piece + trade(piece, (Z7, Z7))
    keep, send = halves(term, inner // 2, 0)
    term = keep + trade(send, (Y2, X2))
    piece = piece + trade(piece, (Z2, Z1))
    piece = piece + trade(after(piece, term), (Z1, Z2))

    other = trade(piece, CORE)
    corner, mixed = jnp.where(core == 0, piece, other), jnp.where(core == 0, other, piece)
    block = 64
    term = term + trade(term, (Z1, Z2))
    term, corner, mixed = lax.optimization_barrier((term, corner, mixed))
    state = factorize_first(corner, mixed, rank, block)
    term = term + trade(term, (Z2, Z1))
    term, *state = lax.optimization_barrier((term, *state))
    factor, inverse = factorize_second(*state, block)
    term = term + trade(term, (Z7, Z7))
    term, factor, inverse = lax.optimization_barrier((term, factor, inverse))
    basis = basis_of(sketched, inverse)
    summed = order(core, term, trade(term, CORE)).reshape(rank, -1)

    row_count = rank // lax.axis_size("gx")
    mine = lax.dynamic_slice_in_dim(inverse, lax.axis_index("gx") * row_count, row_count, 0)
    projection = dot(mine, summed) / total_rows
    return (basis, factor, projection)


def solution(mesh):
    placed = (P(("gx", "gy"), None), P())
    return jax.shard_map(
        body,
        mesh=mesh,
        in_specs=placed,
        out_specs=(P(("gx", "gy"), None), P(), P("gx", "gy")),
        check_vma=False,
    )
```

```python
import functools

import jax
import jax.numpy as jnp
from jax import lax
from jax.experimental import pallas as pl
from jax.experimental.pallas import tpu as pltpu
from jax.sharding import PartitionSpec as P

HIGH = lax.Precision.HIGHEST
F32 = jnp.float32
BF16 = jnp.bfloat16
LIMIT = 60 * 1024 * 1024


def dot(left, right, left_dim=1, right_dim=0, precision=HIGH):
    return lax.dot_general(
        left, right, (((left_dim,), (right_dim,)), ((), ())), precision=precision, preferred_element_type=F32
    )


def square(size):
    row = lax.broadcasted_iota(jnp.int32, (size, size), 0)
    return row, lax.broadcasted_iota(jnp.int32, (size, size), 1)


CHUNKS = 8
SIDE = 4


def mul(left, right):
    return jnp.dot(left, right, preferred_element_type=F32)


def position():
    core, place = lax.axis_index("gx") % 2, lax.axis_index("gy")
    x, y = place % SIDE, place // SIDE
    return core, jnp.where(core == 0, x, y), jnp.where(core == 0, y, x)


def front_kernel(
    rows_hbm, sketch_hbm, sketched_hbm, away_send, away_keep, send, keep,
    rows, sketch, sketched, split, blocks, pieces, row_sems, sketch_sems, sketched_sem, away_sems, own_sems, piece_sems,
    *, scale,
):
    depth = rows.shape[1] // CHUNKS
    rank = sketched.shape[1]
    half, width = blocks.shape[2:]
    core, outer_place, inner_place = position()
    copies = []
    for c in range(CHUNKS):
        part = pl.ds(c * depth, depth)
        pair = (
            pltpu.make_async_copy(sketch_hbm.at[part], sketch.at[part], sketch_sems.at[c]),
            pltpu.make_async_copy(rows_hbm.at[:, part], rows.at[:, part], row_sems.at[c]),
        )
        for copy in pair:
            copy.start()
        copies.append(pair)
    for c in range(CHUNKS):
        for copy in copies[c]:
            copy.wait()
        part = slice(c * depth, (c + 1) * depth)
        term = mul(rows[:, part], sketch[part, :])
        sketched[...] = term if c == 0 else sketched[...] + term
    sketched_copy = pltpu.make_async_copy(sketched, sketched_hbm, sketched_sem)
    sketched_copy.start()

    value = sketched[...]
    high = value.astype(BF16)
    rest = value - high.astype(F32)
    low = rest.astype(BF16)
    last = (rest - low.astype(F32)).astype(BF16)
    turned_high, turned_low = high.T, low.T
    split[:rank, :] = turned_high
    split[rank:, :] = turned_low
    even = mul(turned_high, high) + mul(turned_low, low)
    cross = mul(turned_high, low) + mul(turned_high, last)
    gram = (even + (cross + cross.T)) * scale
    row, col = square(half)
    end = gram[half:, half:]
    diagonal = jnp.sum(jnp.where(row == col, end, 0.0), axis=0, keepdims=True)
    corner, mixed = gram[:half, half:], jnp.where(row <= col, gram[:half, :half], end)
    upper = half // 2
    for at, first in ((0, core == 0), (1, core == 1)):
        value = jnp.where(first, corner, mixed)
        pieces[at, :upper, :half] = value[:upper]
        pieces[at, :upper, half:] = value[upper:]
        pieces[at, upper:, :] = jnp.broadcast_to(jnp.concatenate([diagonal, diagonal], axis=1), (8, rank))
    pieces[2] = jnp.zeros_like(pieces[2])
    tail = pl.ds(SIDE * half, pieces.shape[1])
    tails = []
    for at, ref, side in (
        (0, send, 0), (0, send, 1), (0, keep, 0), (2, keep, 1),
        (1, away_send, 0), (1, away_send, 1), (1, away_keep, 0), (2, away_keep, 1),
    ):
        tails.append(pltpu.make_async_copy(pieces.at[at], ref.at[side, tail], piece_sems.at[len(tails)]))
        tails[-1].start()

    outs = []
    for y in range(SIDE):
        for x in range(SIDE):
            slot = y * SIDE + x
            both = mul(split[...], rows[:, slot * width : (slot + 1) * width])
            both = both[:rank] + both[rank:]
            blocks[0, slot] = both[:half]
            blocks[1, slot] = both[half:]
            for which, bit, refs, sems in (
                (1 - core, inner_place % 2, (away_send, away_keep), away_sems),
                (core, outer_place % 2, (send, keep), own_sems),
            ):
                outer, inner = jnp.where(which == 0, x, y), jnp.where(which == 0, y, x)
                stays = outer % 2 == bit
                for ref, wanted in zip(refs, (jnp.logical_not(stays), stays)):
                    to = ref.at[outer // 2, pl.ds(pl.multiple_of(inner * half, half), half)]
                    copy = pltpu.make_async_copy(blocks.at[which, slot], to, sems.at[slot])
                    pl.when(wanted)(copy.start)
                    outs.append((wanted, copy))
    for wanted, copy in outs:
        pl.when(wanted)(copy.wait)
    sketched_copy.wait()
    for copy in tails:
        copy.wait()


def front(embeddings, sketch, scale):
    count, width = embeddings.shape
    rank = sketch.shape[1]
    half = rank // 2
    hbm = pl.BlockSpec(memory_space=pl.ANY)
    piece = half // 2 + 8
    term = jax.ShapeDtypeStruct((SIDE // 2, SIDE * half + piece, rank), F32)
    return pl.pallas_call(
        functools.partial(front_kernel, scale=scale),
        in_specs=[hbm, hbm],
        out_specs=[hbm] * 5,
        out_shape=[jax.ShapeDtypeStruct((count, rank), F32), term, term, term, term],
        scratch_shapes=[
            pltpu.VMEM((count, width), BF16),
            pltpu.VMEM((width, rank), BF16),
            pltpu.VMEM((count, rank), F32),
            pltpu.VMEM((2 * rank, count), BF16),
            pltpu.VMEM((2, SIDE**2, half, width // SIDE**2), F32),
            pltpu.VMEM((3, piece, rank), F32),
            pltpu.SemaphoreType.DMA((CHUNKS,)),
            pltpu.SemaphoreType.DMA((CHUNKS,)),
            pltpu.SemaphoreType.DMA,
            pltpu.SemaphoreType.DMA((SIDE**2,)),
            pltpu.SemaphoreType.DMA((SIDE**2,)),
            pltpu.SemaphoreType.DMA((8,)),
        ],
        compiler_params=pltpu.CompilerParams(vmem_limit_bytes=LIMIT),
        cost_estimate=pl.CostEstimate(flops=6 * count * width * rank, bytes_accessed=2**24, transcendentals=0),
        name="front",
    )(embeddings, sketch)


def eliminate(pair, size):
    index = lax.broadcasted_iota(jnp.int32, (size, 1), 0)
    lanes = pair.shape[1]
    for j in range(0, size, 8):
        rows = [pair[j + p : j + p + 1, :] for p in range(8)]
        a = {
            (p, q): jnp.broadcast_to(rows[p][:, j + q : j + q + 1], (1, lanes))
            for p in range(8)
            for q in range(p, 8)
        }
        done, steps = [], []
        for s in range(0, 8, 2):
            aa, ab, bb = a[s, s], a[s, s + 1], a[s + 1, s + 1]
            inverse = 1.0 / (aa * bb - ab * ab)
            u, v = rows[s], rows[s + 1]
            top = (bb * u - ab * v) * inverse
            low = (aa * v - ab * u) * inverse
            done += [u, v - (ab / aa) * u]
            cross = {
                q: (
                    (bb * a[s, q] - ab * a[s + 1, q]) * inverse,
                    (aa * a[s + 1, q] - ab * a[s, q]) * inverse,
                )
                for q in range(s + 2, 8)
            }
            for p in range(s + 2, 8):
                rows[p] = rows[p] - (a[s, p] * top + a[s + 1, p] * low)
                for q in range(p, 8):
                    a[p, q] = a[p, q] - (a[s, p] * cross[q][0] + a[s + 1, p] * cross[q][1])
            steps.append((top, low, cross))
        weight = {}
        for s in (6, 4, 2, 0):
            top, low, cross = steps[s // 2]
            for q in range(s + 2, 8):
                top = top - cross[q][0] * weight[q]
                low = low - cross[q][1] * weight[q]
            weight[s], weight[s + 1] = top, low
        if j + 8 == size:
            return jnp.concatenate([pair[:j]] + done, axis=0)
        below = index > j + 7
        total = None
        for p in range(8):
            part = jnp.where(below, pair[:, j + p : j + p + 1], 0.0) * weight[p]
            total = part if total is None else total + part
        rest = pair - total
        pair = jnp.concatenate(([rest[:j]] if j else []) + done + [rest[j + 8 :]], axis=0)
    return pair


def step_blocks(work, upper_ref, blocks, block):
    size = work.shape[0]
    row, col = square(block)
    identity = (row == col).astype(F32)
    for k in blocks:
        lo, hi = k * block, (k + 1) * block
        pair = eliminate(jnp.concatenate([work[lo:hi, lo:hi], identity], axis=1), block)
        diagonal = jnp.sum(jnp.where(row == col, pair[:, :block], 0.0), axis=1, keepdims=True)
        pair = pair * (1.0 / jnp.sqrt(diagonal))
        small = pair[:, block:]
        upper_ref[lo:hi, :] = jnp.where(row <= col, pair[:, :block], 0.0)
        wide = dot(small, work[lo:hi, :])
        left = [wide[:, :lo]] if lo else []
        right = [wide[:, hi:]] if hi < size else []
        wide = jnp.concatenate(left + [small] + right, axis=1)
        if hi < size:
            tall = dot(work[hi:, lo:hi], small, 1, 1)
            lane = lax.broadcasted_iota(jnp.int32, (size - hi, size), 1)
            old = jnp.where((lane >= lo) & (lane < hi), 0.0, work[hi:, :])
            work[hi:, :] = old - dot(tall, wide)
        work[lo:hi, :] = wide


def first_kernel(corner_ref, mixed_ref, work, upper_ref, scales_ref, *, block):
    size = work.shape[0]
    half = size // 2
    row, col = square(half)
    eye = row == col
    upper = half // 2
    corner, mixed = (
        jnp.concatenate([ref[:upper, :half], ref[:upper, half:]]) for ref in (corner_ref, mixed_ref)
    )
    turned = mixed.T
    first = jnp.where(row <= col, mixed, turned)
    last = jnp.where(eye, mixed_ref[upper : upper + 1, :half], jnp.where(row > col, mixed, turned))

    def scales(matrix):
        picked = jnp.where(eye, matrix, 0.0)
        across = jnp.sqrt(jnp.sum(picked, axis=0, keepdims=True))
        down = jnp.sqrt(jnp.sum(picked, axis=1, keepdims=True))
        return across, 1.0 / across, 1.0 / down

    root_a, lane_a, sub_a = scales(first)
    root_b, lane_b, sub_b = scales(last)
    scales_ref[0:1, :] = jnp.concatenate([root_a, root_b], axis=1)
    scales_ref[1:2, :] = jnp.concatenate([lane_a, lane_b], axis=1)
    work[:half, :half] = jnp.where(eye, 1.0, first * sub_a * lane_a)
    work[half:, half:] = jnp.where(eye, 1.0, last * sub_b * lane_b)
    middle = corner * sub_a * lane_b
    work[:half, half:] = middle
    work[half:, :half] = middle.T
    step_blocks(work, upper_ref, range(half // block), block)


def second_kernel(state_ref, upper_ref, scales_ref, factor_ref, inverse_ref, work, upper, *, block):
    size = work.shape[0]
    half = size // 2
    work[...] = state_ref[...]
    upper[:half, :] = upper_ref[:half, :]
    step_blocks(work, upper, range(half // block, size // block), block)
    lane = lax.broadcasted_iota(jnp.int32, (block, size), 1)
    root, back = scales_ref[0:1, :], scales_ref[1:2, :]
    for k in range(size // block):
        lo, hi = k * block, (k + 1) * block
        value = work[lo:hi, :]
        inverse_ref[lo:hi, :] = jnp.where(lane < hi, value, 0.0) * back
        factor_ref[lo:hi, :] = jnp.where(lane >= hi, value, 0.0) * root
        factor_ref[lo:hi, lo:hi] = upper[lo:hi, :] * root[:, lo:hi]


SMALL = 12 * 1024 * 1024


def estimate(microseconds):
    return pl.CostEstimate(flops=microseconds * 2**30, bytes_accessed=2**20, transcendentals=0)


def factorize_first(corner, mixed, size, block):
    return pl.pallas_call(
        functools.partial(first_kernel, block=block),
        out_shape=[
            jax.ShapeDtypeStruct((size, size), F32),
            jax.ShapeDtypeStruct((size, block), F32),
            jax.ShapeDtypeStruct((8, size), F32),
        ],
        compiler_params=pltpu.CompilerParams(vmem_limit_bytes=SMALL),
        cost_estimate=estimate(6),
        name="factorize_first",
    )(corner, mixed)


def factorize_second(state, upper, scales, block):
    size = state.shape[0]
    return pl.pallas_call(
        functools.partial(second_kernel, block=block),
        out_shape=[jax.ShapeDtypeStruct((size, size), F32)] * 2,
        scratch_shapes=[pltpu.VMEM((size, size), F32), pltpu.VMEM((size, block), F32)],
        compiler_params=pltpu.CompilerParams(vmem_limit_bytes=SMALL),
        cost_estimate=estimate(6),
        name="factorize_second",
    )(state, upper, scales)


def basis_kernel(sketched_ref, inverse_ref, basis_ref):
    basis_ref[...] = dot(sketched_ref[...], inverse_ref[...], 1, 1).astype(BF16)


def basis_of(sketched, inverse):
    return pl.pallas_call(
        basis_kernel,
        out_shape=jax.ShapeDtypeStruct(sketched.shape, BF16),
        compiler_params=pltpu.CompilerParams(vmem_limit_bytes=SMALL),
        cost_estimate=estimate(2),
        name="basis",
    )(sketched, inverse)


def trade(value, masks):
    across, along = lax.axis_size("gx"), lax.axis_size("gy")
    pairs = []
    for i in range(across):
        mask_x, mask_y = masks[i % 2]
        for j in range(along):
            pairs.append((i * along + j, (i ^ mask_x) * along + (j ^ mask_y)))
    return lax.ppermute(value, ("gx", "gy"), pairs)


X1, X2, Y1, Y2 = (0, 1), (0, 2), (0, 4), (0, 8)
Z1, Z2, Z6 = (2, 0), (4, 0), (12, 0)
CORE = ((1, 0), (1, 0))


X3, Y3 = (0, 3), (0, 12)


def halves(value, bit, dim):
    keep = lax.dynamic_index_in_dim(value, bit, dim, keepdims=False)
    return keep, lax.dynamic_index_in_dim(value, 1 - bit, dim, keepdims=False)


def trade_both(value, piece, masks):
    flat = value.reshape(-1, piece.shape[1])
    got = trade(jnp.concatenate([flat, piece]), masks)
    return got[: flat.shape[0]].reshape(value.shape), got[flat.shape[0] :]


def after(value, *others):
    return lax.optimization_barrier((value, *others))[0]


def order(core, mine, other):
    return jnp.where(core == 0, jnp.stack([mine, other]), jnp.stack([other, mine]))


def body(embeddings, sketch):
    total_rows = embeddings.shape[0] * lax.axis_size("gx") * lax.axis_size("gy")
    rank = sketch.shape[1]
    core, outer, inner = position()
    sketched, away_send, away_keep, send, keep = front(embeddings, sketch, 1.0 / total_rows)
    half = rank // 2
    rows = SIDE * half

    got = trade(away_send, CORE)
    message = [send[side] + got[side] for side in range(2)]
    keep = keep + trade(after(away_keep, message[0]), CORE)
    one = keep[0] + trade(message[0], (X1, Y1))
    three = keep[1] + trade(message[1], (X3, Y3))
    piece = one[rows:] + (trade(message[0][rows:], (X2, Y2)) + three[rows:])
    terms = [part[:rows].reshape(2, 2, half, -1) for part in (one, three)]
    parts = [halves(term, inner % 2, 1) for term in terms]
    one, piece_1 = trade_both(parts[0][1], piece, (Y1, X1))
    three, piece_3 = trade_both(parts[1][1], piece, (Y3, X3))
    piece = (piece + piece_1) + (trade(piece, (Y2, X2)) + piece_3)
    low, high = (part[0] + got for part, got in zip(parts, (one, three)))
    upper = outer // 2 == 1
    term = jnp.where(upper, high, low) + trade(jnp.where(upper, low, high), (X2, Y2))
    piece = piece + trade(piece, (Z6, Z6))
    keep, send = halves(term, inner // 2, 0)
    term = keep + trade(send, (Y2, X2))
    piece = piece + trade(piece, (Z2, Z1))
    piece = piece + trade(after(piece, term), (Z1, Z2))

    other = trade(piece, CORE)
    corner, mixed = jnp.where(core == 0, piece, other), jnp.where(core == 0, other, piece)
    block = 128
    term = term + trade(term, (Z1, Z2))
    term, corner, mixed = lax.optimization_barrier((term, corner, mixed))
    state = factorize_first(corner, mixed, rank, block)
    term = term + trade(term, (Z2, Z1))
    term, *state = lax.optimization_barrier((term, *state))
    factor, inverse = factorize_second(*state, block)
    term = term + trade(term, (Z6, Z6))
    term, factor, inverse = lax.optimization_barrier((term, factor, inverse))
    basis = basis_of(sketched, inverse)
    summed = order(core, term, trade(term, CORE)).reshape(rank, -1)

    row_count = rank // lax.axis_size("gx")
    mine = lax.dynamic_slice_in_dim(inverse, lax.axis_index("gx") * row_count, row_count, 0)
    projection = dot(mine, summed) / total_rows
    return (basis, factor, projection)


def solution(mesh):
    placed = (P(("gx", "gy"), None), P())
    return jax.shard_map(
        body,
        mesh=mesh,
        in_specs=placed,
        out_specs=(P(("gx", "gy"), None), P(), P("gx", "gy")),
        check_vma=False,
    )
```

```python
import functools

import jax
import jax.numpy as jnp
from jax import lax
from jax.experimental import pallas as pl
from jax.experimental.pallas import tpu as pltpu
from jax.sharding import PartitionSpec as P

HIGH = lax.Precision.HIGHEST
F32 = jnp.float32
BF16 = jnp.bfloat16
LIMIT = 60 * 1024 * 1024


def dot(left, right, left_dim=1, right_dim=0, precision=HIGH):
    return lax.dot_general(
        left, right, (((left_dim,), (right_dim,)), ((), ())), precision=precision, preferred_element_type=F32
    )


def square(size):
    row = lax.broadcasted_iota(jnp.int32, (size, size), 0)
    return row, lax.broadcasted_iota(jnp.int32, (size, size), 1)


CHUNKS = 8
SIDE = 4


def mul(left, right):
    return jnp.dot(left, right, preferred_element_type=F32)


def position():
    core, place = lax.axis_index("gx") % 2, lax.axis_index("gy")
    x, y = place % SIDE, place // SIDE
    return core, jnp.where(core == 0, x, y), jnp.where(core == 0, y, x)


def front_kernel(
    rows_hbm, sketch_hbm, sketched_hbm, away_send, away_keep, send, keep,
    rows, sketch, sketched, split, blocks, pieces, row_sems, sketch_sems, sketched_sem, away_sems, own_sems, piece_sems,
    *, scale,
):
    depth = rows.shape[1] // CHUNKS
    rank = sketched.shape[1]
    half, width = blocks.shape[2:]
    core, outer_place, inner_place = position()
    copies = []
    for c in range(CHUNKS):
        part = pl.ds(c * depth, depth)
        pair = (
            pltpu.make_async_copy(sketch_hbm.at[part], sketch.at[part], sketch_sems.at[c]),
            pltpu.make_async_copy(rows_hbm.at[:, part], rows.at[:, part], row_sems.at[c]),
        )
        for copy in pair:
            copy.start()
        copies.append(pair)
    for c in range(CHUNKS):
        for copy in copies[c]:
            copy.wait()
        part = slice(c * depth, (c + 1) * depth)
        term = mul(rows[:, part], sketch[part, :])
        sketched[...] = term if c == 0 else sketched[...] + term
    sketched_copy = pltpu.make_async_copy(sketched, sketched_hbm, sketched_sem)
    sketched_copy.start()

    value = sketched[...]
    high = value.astype(BF16)
    rest = value - high.astype(F32)
    low = rest.astype(BF16)
    last = (rest - low.astype(F32)).astype(BF16)
    turned_high, turned_low = high.T, low.T
    split[:rank, :] = turned_high
    split[rank:, :] = turned_low
    even = mul(turned_high, high) + mul(turned_low, low)
    cross = mul(turned_high, low) + mul(turned_high, last)
    gram = (even + (cross + cross.T)) * scale
    row, col = square(half)
    end = gram[half:, half:]
    diagonal = jnp.sum(jnp.where(row == col, end, 0.0), axis=0, keepdims=True)
    corner, mixed = gram[:half, half:], jnp.where(row <= col, gram[:half, :half], end)
    upper = half // 2
    for at, first in ((0, core == 0), (1, core == 1)):
        value = jnp.where(first, corner, mixed)
        pieces[at, :upper, :half] = value[:upper]
        pieces[at, :upper, half:] = value[upper:]
        pieces[at, upper:, :] = jnp.broadcast_to(jnp.concatenate([diagonal, diagonal], axis=1), (8, rank))
    pieces[2] = jnp.zeros_like(pieces[2])
    tail = pl.ds(SIDE * half, pieces.shape[1])
    tails = []
    for at, ref, side in (
        (0, send, 0), (0, send, 1), (0, keep, 0), (2, keep, 1),
        (1, away_send, 0), (1, away_send, 1), (1, away_keep, 0), (2, away_keep, 1),
    ):
        tails.append(pltpu.make_async_copy(pieces.at[at], ref.at[side, tail], piece_sems.at[len(tails)]))
        tails[-1].start()

    outs = []
    for y in range(SIDE):
        for x in range(SIDE):
            slot = y * SIDE + x
            both = mul(split[...], rows[:, slot * width : (slot + 1) * width])
            both = both[:rank] + both[rank:]
            blocks[0, slot] = both[:half]
            blocks[1, slot] = both[half:]
            for which, bit, refs, sems in (
                (1 - core, inner_place % 2, (away_send, away_keep), away_sems),
                (core, outer_place % 2, (send, keep), own_sems),
            ):
                outer, inner = jnp.where(which == 0, x, y), jnp.where(which == 0, y, x)
                stays = outer % 2 == bit
                for ref, wanted in zip(refs, (jnp.logical_not(stays), stays)):
                    to = ref.at[outer // 2, pl.ds(pl.multiple_of(inner * half, half), half)]
                    copy = pltpu.make_async_copy(blocks.at[which, slot], to, sems.at[slot])
                    pl.when(wanted)(copy.start)
                    outs.append((wanted, copy))
    for wanted, copy in outs:
        pl.when(wanted)(copy.wait)
    sketched_copy.wait()
    for copy in tails:
        copy.wait()


def front(embeddings, sketch, scale):
    count, width = embeddings.shape
    rank = sketch.shape[1]
    half = rank // 2
    hbm = pl.BlockSpec(memory_space=pl.ANY)
    piece = half // 2 + 8
    term = jax.ShapeDtypeStruct((SIDE // 2, SIDE * half + piece, rank), F32)
    return pl.pallas_call(
        functools.partial(front_kernel, scale=scale),
        in_specs=[hbm, hbm],
        out_specs=[hbm] * 5,
        out_shape=[jax.ShapeDtypeStruct((count, rank), F32), term, term, term, term],
        scratch_shapes=[
            pltpu.VMEM((count, width), BF16),
            pltpu.VMEM((width, rank), BF16),
            pltpu.VMEM((count, rank), F32),
            pltpu.VMEM((2 * rank, count), BF16),
            pltpu.VMEM((2, SIDE**2, half, width // SIDE**2), F32),
            pltpu.VMEM((3, piece, rank), F32),
            pltpu.SemaphoreType.DMA((CHUNKS,)),
            pltpu.SemaphoreType.DMA((CHUNKS,)),
            pltpu.SemaphoreType.DMA,
            pltpu.SemaphoreType.DMA((SIDE**2,)),
            pltpu.SemaphoreType.DMA((SIDE**2,)),
            pltpu.SemaphoreType.DMA((8,)),
        ],
        compiler_params=pltpu.CompilerParams(vmem_limit_bytes=LIMIT),
        cost_estimate=pl.CostEstimate(flops=6 * count * width * rank, bytes_accessed=2**24, transcendentals=0),
        name="front",
    )(embeddings, sketch)


def eliminate(pair, size):
    index = lax.broadcasted_iota(jnp.int32, (size, 1), 0)
    lanes = pair.shape[1]
    for j in range(0, size, 8):
        rows = [pair[j + p : j + p + 1, :] for p in range(8)]
        a = {
            (p, q): jnp.broadcast_to(rows[p][:, j + q : j + q + 1], (1, lanes))
            for p in range(8)
            for q in range(p, 8)
        }
        done, steps = [], []
        for s in range(0, 8, 2):
            aa, ab, bb = a[s, s], a[s, s + 1], a[s + 1, s + 1]
            inverse = 1.0 / (aa * bb - ab * ab)
            u, v = rows[s], rows[s + 1]
            top = (bb * u - ab * v) * inverse
            low = (aa * v - ab * u) * inverse
            done += [u, v - (ab / aa) * u]
            cross = {
                q: (
                    (bb * a[s, q] - ab * a[s + 1, q]) * inverse,
                    (aa * a[s + 1, q] - ab * a[s, q]) * inverse,
                )
                for q in range(s + 2, 8)
            }
            for p in range(s + 2, 8):
                rows[p] = rows[p] - (a[s, p] * top + a[s + 1, p] * low)
                for q in range(p, 8):
                    a[p, q] = a[p, q] - (a[s, p] * cross[q][0] + a[s + 1, p] * cross[q][1])
            steps.append((top, low, cross))
        weight = {}
        for s in (6, 4, 2, 0):
            top, low, cross = steps[s // 2]
            for q in range(s + 2, 8):
                top = top - cross[q][0] * weight[q]
                low = low - cross[q][1] * weight[q]
            weight[s], weight[s + 1] = top, low
        if j + 8 == size:
            return jnp.concatenate([pair[:j]] + done, axis=0)
        below = index > j + 7
        total = None
        for p in range(8):
            part = jnp.where(below, pair[:, j + p : j + p + 1], 0.0) * weight[p]
            total = part if total is None else total + part
        rest = pair - total
        pair = jnp.concatenate(([rest[:j]] if j else []) + done + [rest[j + 8 :]], axis=0)
    return pair


def step_blocks(work, upper_ref, blocks, block):
    size = work.shape[0]
    row, col = square(block)
    identity = (row == col).astype(F32)
    for k in blocks:
        lo, hi = k * block, (k + 1) * block
        pair = eliminate(jnp.concatenate([work[lo:hi, lo:hi], identity], axis=1), block)
        diagonal = jnp.sum(jnp.where(row == col, pair[:, :block], 0.0), axis=1, keepdims=True)
        pair = pair * (1.0 / jnp.sqrt(diagonal))
        small = pair[:, block:]
        upper_ref[lo:hi, :] = jnp.where(row <= col, pair[:, :block], 0.0)
        wide = dot(small, work[lo:hi, :])
        left = [wide[:, :lo]] if lo else []
        right = [wide[:, hi:]] if hi < size else []
        wide = jnp.concatenate(left + [small] + right, axis=1)
        if hi < size:
            tall = dot(work[hi:, lo:hi], small, 1, 1)
            lane = lax.broadcasted_iota(jnp.int32, (size - hi, size), 1)
            old = jnp.where((lane >= lo) & (lane < hi), 0.0, work[hi:, :])
            work[hi:, :] = old - dot(tall, wide)
        work[lo:hi, :] = wide


def first_kernel(corner_ref, mixed_ref, work, upper_ref, scales_ref, *, block):
    size = work.shape[0]
    half = size // 2
    row, col = square(half)
    eye = row == col
    upper = half // 2
    corner, mixed = (
        jnp.concatenate([ref[:upper, :half], ref[:upper, half:]]) for ref in (corner_ref, mixed_ref)
    )
    turned = mixed.T
    first = jnp.where(row <= col, mixed, turned)
    last = jnp.where(eye, mixed_ref[upper : upper + 1, :half], jnp.where(row > col, mixed, turned))

    def scales(matrix):
        picked = jnp.where(eye, matrix, 0.0)
        across = jnp.sqrt(jnp.sum(picked, axis=0, keepdims=True))
        down = jnp.sqrt(jnp.sum(picked, axis=1, keepdims=True))
        return across, 1.0 / across, 1.0 / down

    root_a, lane_a, sub_a = scales(first)
    root_b, lane_b, sub_b = scales(last)
    scales_ref[0:1, :] = jnp.concatenate([root_a, root_b], axis=1)
    scales_ref[1:2, :] = jnp.concatenate([lane_a, lane_b], axis=1)
    work[:half, :half] = jnp.where(eye, 1.0, first * sub_a * lane_a)
    work[half:, half:] = jnp.where(eye, 1.0, last * sub_b * lane_b)
    middle = corner * sub_a * lane_b
    work[:half, half:] = middle
    work[half:, :half] = middle.T
    step_blocks(work, upper_ref, range(half // block), block)


def second_kernel(state_ref, upper_ref, scales_ref, factor_ref, inverse_ref, work, upper, *, block):
    size = work.shape[0]
    half = size // 2
    work[...] = state_ref[...]
    upper[:half, :] = upper_ref[:half, :]
    step_blocks(work, upper, range(half // block, size // block), block)
    lane = lax.broadcasted_iota(jnp.int32, (block, size), 1)
    root, back = scales_ref[0:1, :], scales_ref[1:2, :]
    for k in range(size // block):
        lo, hi = k * block, (k + 1) * block
        value = work[lo:hi, :]
        inverse_ref[lo:hi, :] = jnp.where(lane < hi, value, 0.0) * back
        factor_ref[lo:hi, :] = jnp.where(lane >= hi, value, 0.0) * root
        factor_ref[lo:hi, lo:hi] = upper[lo:hi, :] * root[:, lo:hi]


SMALL = 12 * 1024 * 1024


def estimate(microseconds):
    return pl.CostEstimate(flops=microseconds * 2**30, bytes_accessed=2**20, transcendentals=0)


def factorize_first(corner, mixed, size, block):
    return pl.pallas_call(
        functools.partial(first_kernel, block=block),
        out_shape=[
            jax.ShapeDtypeStruct((size, size), F32),
            jax.ShapeDtypeStruct((size, block), F32),
            jax.ShapeDtypeStruct((8, size), F32),
        ],
        compiler_params=pltpu.CompilerParams(vmem_limit_bytes=SMALL),
        cost_estimate=estimate(6),
        name="factorize_first",
    )(corner, mixed)


def factorize_second(state, upper, scales, block):
    size = state.shape[0]
    return pl.pallas_call(
        functools.partial(second_kernel, block=block),
        out_shape=[jax.ShapeDtypeStruct((size, size), F32)] * 2,
        scratch_shapes=[pltpu.VMEM((size, size), F32), pltpu.VMEM((size, block), F32)],
        compiler_params=pltpu.CompilerParams(vmem_limit_bytes=SMALL),
        cost_estimate=estimate(6),
        name="factorize_second",
    )(state, upper, scales)


def basis_kernel(sketched_ref, inverse_ref, basis_ref):
    basis_ref[...] = dot(sketched_ref[...], inverse_ref[...], 1, 1).astype(BF16)


def basis_of(sketched, inverse):
    return pl.pallas_call(
        basis_kernel,
        out_shape=jax.ShapeDtypeStruct(sketched.shape, BF16),
        compiler_params=pltpu.CompilerParams(vmem_limit_bytes=SMALL),
        cost_estimate=estimate(2),
        name="basis",
    )(sketched, inverse)


def trade(value, masks):
    across, along = lax.axis_size("gx"), lax.axis_size("gy")
    pairs = []
    for i in range(across):
        mask_x, mask_y = masks[i % 2]
        for j in range(along):
            pairs.append((i * along + j, (i ^ mask_x) * along + (j ^ mask_y)))
    return lax.ppermute(value, ("gx", "gy"), pairs)


X1, X2, Y1, Y2 = (0, 1), (0, 2), (0, 4), (0, 8)
Z1, Z2, Z6 = (2, 0), (4, 0), (12, 0)
CORE = ((1, 0), (1, 0))


X3, Y3 = (0, 3), (0, 12)


def halves(value, bit, dim):
    keep = lax.dynamic_index_in_dim(value, bit, dim, keepdims=False)
    return keep, lax.dynamic_index_in_dim(value, 1 - bit, dim, keepdims=False)


def trade_both(value, piece, masks):
    flat = value.reshape(-1, piece.shape[1])
    got = trade(jnp.concatenate([flat, piece]), masks)
    return got[: flat.shape[0]].reshape(value.shape), got[flat.shape[0] :]


def after(value, *others):
    return lax.optimization_barrier((value, *others))[0]


def order(core, mine, other):
    return jnp.where(core == 0, jnp.stack([mine, other]), jnp.stack([other, mine]))


def body(embeddings, sketch):
    total_rows = embeddings.shape[0] * lax.axis_size("gx") * lax.axis_size("gy")
    rank = sketch.shape[1]
    core, outer, inner = position()
    sketched, away_send, away_keep, send, keep = front(embeddings, sketch, 1.0 / total_rows)
    half = rank // 2
    rows = SIDE * half

    message = send + trade(away_send, CORE)
    keep = keep + trade(after(away_keep, message), CORE)
    one = keep[0] + trade(message[0], (X1, Y1))
    three = keep[1] + trade(message[1], (X3, Y3))
    piece = one[rows:] + (trade(message[0, rows:], (X2, Y2)) + three[rows:])
    terms = [part[:rows].reshape(2, 2, half, -1) for part in (one, three)]
    parts = [halves(term, inner % 2, 1) for term in terms]
    one, piece_1 = trade_both(parts[0][1], piece, (Y1, X1))
    three, piece_3 = trade_both(parts[1][1], piece, (Y3, X3))
    piece = (piece + piece_1) + (trade(piece, (Y2, X2)) + piece_3)
    low, high = (part[0] + got for part, got in zip(parts, (one, three)))
    upper = outer // 2 == 1
    term = jnp.where(upper, high, low) + trade(jnp.where(upper, low, high), (X2, Y2))
    piece = piece + trade(piece, (Z6, Z6))
    keep, send = halves(term, inner // 2, 0)
    term = keep + trade(send, (Y2, X2))
    piece = piece + trade(piece, (Z2, Z1))
    piece = piece + trade(after(piece, term), (Z1, Z2))

    other = trade(piece, CORE)
    corner, mixed = jnp.where(core == 0, piece, other), jnp.where(core == 0, other, piece)
    block = 128
    term = term + trade(term, (Z1, Z2))
    term, corner, mixed = lax.optimization_barrier((term, corner, mixed))
    state = factorize_first(corner, mixed, rank, block)
    term = term + trade(term, (Z2, Z1))
    term, *state = lax.optimization_barrier((term, *state))
    factor, inverse = factorize_second(*state, block)
    term = term + trade(term, (Z6, Z6))
    term, factor, inverse = lax.optimization_barrier((term, factor, inverse))
    basis = basis_of(sketched, inverse)
    summed = order(core, term, trade(term, CORE)).reshape(rank, -1)

    row_count = rank // lax.axis_size("gx")
    mine = lax.dynamic_slice_in_dim(inverse, lax.axis_index("gx") * row_count, row_count, 0)
    projection = dot(mine, summed) / total_rows
    return (basis, factor, projection)


def solution(mesh):
    placed = (P(("gx", "gy"), None), P())
    return jax.shard_map(
        body,
        mesh=mesh,
        in_specs=placed,
        out_specs=(P(("gx", "gy"), None), P(), P("gx", "gy")),
        check_vma=False,
    )
```
